32 devices in a mesh: dp: 8 (over y, x, core), mp: 4 (over z).
Axes of the slice: x: 2, y: 2, z: 4, core: 2. Of those that a mesh axis runs over, the one named last changes fastest.
Arguments:
- gradients: bfloat16 [8, 2, 8192, 1024], P('dp', None, None, 'mp'), may hold values from -16 to 16
- feedback: bfloat16 [8, 2, 8192, 1024], P('dp', None, None, 'mp'), may hold values from -1.796875 to 1.796875
- right_factor: float32 [2, 1024, 16], P(None, 'mp'), may hold values from -6 to 6
Outputs:
- new_feedback: bfloat16 [8, 2, 8192, 1024], P('dp', None, None, 'mp')
- update: bfloat16 [2, 8192, 1024], P(None, 'dp', 'mp')
The draws below stay inside these ranges and needn't reach their ends.
All inputs are finite; a program needn't handle non-finite values.
Results may differ from the reference program's by a relative error of at most 0.0095.
Values may be sent and summed in bfloat16 or wider, within the bound.
A program may use at most 64 MiB of HBM per device.

```python
import math
import jax
import jax.numpy as jnp
from jax import lax

D = 8192
KV = 1024
RANK = 16
MATS = 2
REPLICAS = 8


def draw_gradients(key, part):
    subkeys = jax.random.split(key, 8)
    basis_width = RANK + 8
    left_basis = jax.random.normal(subkeys[0], (MATS, D, basis_width), jnp.float32)
    right_basis = jax.random.normal(subkeys[1], (MATS, KV, basis_width), jnp.float32)
    spreads = jnp.exp(jax.random.uniform(subkeys[2], (MATS, basis_width), jnp.float32, 0.0, math.log(8.0)))
    shared_part = jnp.einsum('mdw,mcw->mdc', left_basis * spreads[:, None, :], right_basis)
    shared_part = shared_part / jnp.sqrt(jnp.sum(spreads * spreads, axis=1))[:, None, None]
    own_left = jax.random.normal(subkeys[4], (REPLICAS, MATS, D, 4), jnp.float32)
    own_right = jax.random.normal(subkeys[5], (REPLICAS, MATS, KV, 4), jnp.float32)
    own_part = jnp.einsum('imdw,imcw->imdc', own_left, own_right) / 2.0
    pairing = jax.random.permutation(subkeys[6], REPLICAS)
    row_block = jnp.arange(D) // (D // REPLICAS)
    boosted = jnp.where(row_block[None, :] == pairing[:, None], 6.0, 1.0)
    noise_part = 0.3 * jax.random.normal(subkeys[7], (REPLICAS, MATS, D, KV), jnp.float32)
    combined = shared_part[None] + own_part * boosted[:, None, :, None] + noise_part
    return jnp.clip(combined, -16.0, 16.0).astype(jnp.bfloat16)


def block_levels(own_key, extent, pieces, least, high):
    gain = 1.0
    for position, blocks in pieces:
        heights = jax.random.uniform(jax.random.fold_in(jax.random.fold_in(own_key, 6), position), (blocks,), jnp.float32, least / len(pieces), high / len(pieces))
        gain = gain * jnp.repeat(jnp.exp(heights), extent[position] // blocks).reshape((-1,) + (1,) * (len(extent) - 1 - position))
    return gain


def scatter_about(stream_key, shape, spread, bound, cuts=(), dtype=jnp.bfloat16):
    level = block_levels(stream_key, shape, cuts, -0.22, 0.18) if cuts else 1.0
    entries = jax.random.normal(stream_key, shape, jnp.float32) * spread * level
    return jnp.minimum(jnp.maximum(entries, -bound), bound).astype(dtype)


def setup_inputs(seed: int = 0) -> dict:
    streams_of = jax.random.split(jax.random.key(seed), 4)
    gradients = draw_gradients(jax.random.fold_in(streams_of[3], 71), 0)
    feedback = scatter_about(streams_of[1], (REPLICAS, MATS, D, KV), 0.3, 1.796875, ((0, 8), (3, 4)))
    right_factor = scatter_about(streams_of[2], (MATS, KV, RANK), 1.0, 6.0, ((1, 4),), jnp.float32)
    return dict(gradients=gradients, feedback=feedback, right_factor=right_factor)


def orthonormal(left_total):
    gram_matrix = jnp.einsum('mdr,mds->mrs', left_total, left_total, precision=lax.Precision.HIGHEST)
    lower_factor = jnp.linalg.cholesky(gram_matrix)
    return lax.linalg.triangular_solve(lower_factor, left_total, left_side=False, lower=True, transpose_a=True)

def compensate(gradient_piece, feedback_piece):
    summed = (gradient_piece.astype(jnp.float32) + feedback_piece.astype(jnp.float32)).astype(jnp.bfloat16)
    return lax.optimization_barrier(summed).astype(jnp.float32)

def reference(gradients, feedback, right_factor):
    right_start = lax.optimization_barrier(right_factor.astype(jnp.bfloat16)).astype(jnp.float32)

    def add_left(running, pair_items):
        compensated = compensate(pair_items[0], pair_items[1])
        term = jnp.einsum('mdc,mcr->mdr', compensated, right_start, precision=lax.Precision.HIGHEST)
        return (running + term / REPLICAS, None)
    left_total, _ = lax.scan(add_left, jnp.zeros((MATS, D, RANK), jnp.float32), (gradients, feedback))
    left_low = lax.optimization_barrier(orthonormal(left_total).astype(jnp.bfloat16)).astype(jnp.float32)

    def add_right(running, pair_items):
        compensated = compensate(pair_items[0], pair_items[1])
        term = jnp.einsum('mdc,mdr->mcr', compensated, left_low, precision=lax.Precision.HIGHEST)
        return (running + term / REPLICAS, None)
    right_total, _ = lax.scan(add_right, jnp.zeros((MATS, KV, RANK), jnp.float32), (gradients, feedback))
    right_low = lax.optimization_barrier(right_total.astype(jnp.bfloat16)).astype(jnp.float32)
    approx = jnp.einsum('mdr,mcr->mdc', left_low, right_low, precision=lax.Precision.HIGHEST)

    def residue(carried, pair_items):
        compensated = compensate(pair_items[0], pair_items[1])
        return (carried, (compensated - approx).astype(jnp.bfloat16))
    _, new_feedback = lax.scan(residue, jnp.zeros((), jnp.float32), (gradients, feedback))
    return (new_feedback, approx.astype(jnp.bfloat16))
```

```python
import functools

import jax
import jax.numpy as jnp
from jax import lax
from jax.experimental import pallas as pl
from jax.experimental.pallas import tpu as pltpu
from jax.sharding import PartitionSpec as P

LANES = 128
CORES = 2
F32 = jnp.float32
BF16 = jnp.bfloat16


def split3(value):
    high = value.astype(BF16)
    rest = value - high.astype(F32)
    middle = rest.astype(BF16)
    low = (rest - middle.astype(F32)).astype(BF16)
    return high, middle, low


def nt_dot(left, right):
    return lax.dot_general(left, right, (((1,), (1,)), ((), ())), preferred_element_type=F32)


def nn_dot(left, right):
    return lax.dot_general(left, right, (((1,), (0,)), ((), ())), preferred_element_type=F32)


def reduce_kernel(
    n_dp, n_mp,
    grad_hbm, feed_hbm, right_ref,
    comp_hbm, q_hbm, right_low_ref,
    comp, feed, part, half, from_core, from_chip, plane, from_z, full,
    gram_chip, gram_core, q_low, right_all,
    load_sem, store_sem, qstore_sem,
    core_send, core_recv, chip_send, chip_recv, z_send, z_recv,
    zg_send, zg_recv, cg_send, cg_recv, kg_send, kg_recv,
    gc_send, gc_recv, gk_send, gk_recv, r_send, r_recv,
):
    mats, rows, cols = comp.shape
    rank = right_ref.shape[2]
    blocks = rows // LANES
    tile = q_low.shape[3]
    tiles = rows // tile
    per_tile = tile // LANES
    chips = n_dp // CORES
    half_blocks = blocks // CORES
    chip_blocks = half_blocks // chips
    z_split = chip_blocks % n_mp == 0
    z_blocks = chip_blocks // n_mp if z_split else chip_blocks

    dp = lax.axis_index("dp")
    z = lax.axis_index("mp")
    core = lax.rem(dp, CORES)
    chip = dp // CORES
    other = 1 - core
    twin = chip * CORES + other

    def loads(m, t):
        span = pl.ds(t * tile, tile)
        return (
            pltpu.make_async_copy(grad_hbm.at[0, m, span], comp.at[m, span], load_sem.at[0, m, t]),
            pltpu.make_async_copy(feed_hbm.at[0, m, span], feed.at[m, span], load_sem.at[1, m, t]),
        )

    for m in range(mats):
        def start_loads(t, carry, m=m):
            for copy in loads(m, t):
                copy.start()
            return carry
        lax.fori_loop(0, tiles, start_loads, 0)

    barrier = pltpu.get_barrier_semaphore()
    for k in range(1, n_dp):
        pl.semaphore_signal(barrier, inc=1, device_id=(lax.rem(dp + k, n_dp), z),
                            device_id_type=pl.DeviceIdType.MESH)
    for k in range(1, n_mp):
        pl.semaphore_signal(barrier, inc=1, device_id=(dp, lax.rem(z + k, n_mp)),
                            device_id_type=pl.DeviceIdType.MESH)
    pl.semaphore_wait(barrier, n_dp - 1 + n_mp - 1)

    sent = []

    def remote(src, dst, send_sem, recv_sem, device):
        return pltpu.make_async_remote_copy(
            src_ref=src, dst_ref=dst, send_sem=send_sem, recv_sem=recv_sem,
            device_id=device, device_id_type=pl.DeviceIdType.MESH)

    def send(*args):
        copy = remote(*args)
        copy.start()
        sent.append(copy)

    def landed(dst, send_sem, recv_sem):
        remote(dst, dst, send_sem, recv_sem, (twin, z)).wait_recv()

    eye = (lax.broadcasted_iota(jnp.int32, (rank, rank), 0)
           == lax.broadcasted_iota(jnp.int32, (rank, rank), 1)).astype(BF16)

    def compensate(m, first, last):
        right_t = nt_dot(eye, right_ref[m].astype(BF16)).astype(BF16)

        def body(t, carry):
            for copy in loads(m, t):
                copy.wait()
            span = pl.ds(pl.multiple_of(t * tile, tile), tile)
            value = (comp[m, span].astype(F32) + feed[m, span].astype(F32)).astype(BF16)
            comp[m, span] = value
            term = nt_dot(right_t, value)
            for j in range(per_tile):
                part[m, t * per_tile + j] = term[:, j * LANES:(j + 1) * LANES]
            pltpu.make_async_copy(comp.at[m, span], comp_hbm.at[m, span], store_sem.at[m, t]).start()
            return carry
        lax.fori_loop(first, last, body, 0)

    def core_start(m):
        send(part.at[m, pl.ds(other * half_blocks, half_blocks)], from_core.at[m],
             core_send.at[m], core_recv.at[m], (twin, z))

    def core_finish(m):
        landed(from_core.at[m], core_send.at[m], core_recv.at[m])
        half[m] = part[m, pl.ds(core * half_blocks, half_blocks)] + from_core[m]

    def chip_start(m):
        for k in range(1, chips):
            to = lax.rem(chip + k, chips)
            send(half.at[m, pl.ds(to * chip_blocks, chip_blocks)], from_chip.at[m, chip],
                 chip_send.at[m, k], chip_recv.at[m, chip], (to * CORES + core, z))

    def chip_finish(m):
        total = half[m, pl.ds(chip * chip_blocks, chip_blocks)]
        for k in range(1, chips):
            source = lax.rem(chip + k, chips)
            landed(from_chip.at[m, source], chip_send.at[m, k], chip_recv.at[m, source])
            total = total + from_chip[m, source]
        plane[m] = total

    def z_start(m):
        for k in range(1, n_mp):
            to = lax.rem(z + k, n_mp)
            first = to * z_blocks if z_split else 0
            send(plane.at[m, pl.ds(first, z_blocks)], from_z.at[m, z],
                 z_send.at[m, k], z_recv.at[m, z], (dp, to))

    base = core * half_blocks + chip * chip_blocks
    mine = pl.ds(base + (z * z_blocks if z_split else 0), z_blocks)

    def z_finish(m):
        total = plane[m, pl.ds(z * z_blocks if z_split else 0, z_blocks)]
        for k in range(1, n_mp):
            source = lax.rem(z + k, n_mp)
            landed(from_z.at[m, source], z_send.at[m, k], z_recv.at[m, source])
            total = total + from_z[m, source]
        full[m, mine] = total * (1.0 / n_dp)

    def z_gather_start(m):
        if z_split:
            for k in range(1, n_mp):
                send(full.at[m, mine], full.at[m, mine], zg_send.at[m, k], zg_recv.at[m, z],
                     (dp, lax.rem(z + k, n_mp)))

    def z_gather_finish(m):
        if z_split:
            for k in range(1, n_mp):
                source = lax.rem(z + k, n_mp)
                landed(full.at[m, pl.ds(base + source * z_blocks, z_blocks)],
                       zg_send.at[m, k], zg_recv.at[m, source])

    gram_lane = 6 * rank

    def chip_gather_start(m):
        own = pl.ds(base, chip_blocks)
        for k in range(1, chips):
            to = lax.rem(chip + k, chips)
            send(full.at[m, own], full.at[m, own], cg_send.at[m, k], cg_recv.at[m, chip],
                 (to * CORES + core, z))
        value = jnp.concatenate([full[m, base + j] for j in range(chip_blocks)], axis=1)
        terms = split3(value)
        tall = jnp.concatenate(terms, axis=0)
        pad = jnp.zeros((gram_lane, value.shape[1]), BF16)
        wide = sum(nt_dot(tall, jnp.concatenate([pad, term], axis=0)) for term in terms)
        gram = wide[0:rank] + wide[rank:2 * rank] + wide[2 * rank:3 * rank]
        gram_chip[m, chip] = jnp.zeros((rank, LANES), F32)
        gram_chip[m, chip, :, 0:gram_lane + rank] = gram
        for k in range(1, chips):
            to = lax.rem(chip + k, chips)
            send(gram_chip.at[m, chip], gram_chip.at[m, chip], gc_send.at[m, k],
                 gc_recv.at[m, chip], (to * CORES + core, z))

    def chip_gather_finish(m):
        for k in range(1, chips):
            source = lax.rem(chip + k, chips)
            landed(full.at[m, pl.ds(core * half_blocks + source * chip_blocks, chip_blocks)],
                   cg_send.at[m, k], cg_recv.at[m, source])
            landed(gram_chip.at[m, source], gc_send.at[m, k], gc_recv.at[m, source])

    def core_gather_start(m):
        own = pl.ds(core * half_blocks, half_blocks)
        send(full.at[m, own], full.at[m, own], kg_send.at[m], kg_recv.at[m], (twin, z))
        total = gram_chip[m, 0]
        for c in range(1, chips):
            total = total + gram_chip[m, c]
        gram_core[m, core] = total
        send(gram_core.at[m, core], gram_core.at[m, core], gk_send.at[m], gk_recv.at[m], (twin, z))

    def core_gather_finish(m):
        landed(gram_core.at[m, other], gk_send.at[m], gk_recv.at[m])
        landed(full.at[m, pl.ds(other * half_blocks, half_blocks)], kg_send.at[m], kg_recv.at[m])

    row_at = lax.broadcasted_iota(jnp.int32, (rank, LANES), 0)
    lane_at = lax.broadcasted_iota(jnp.int32, (rank, LANES), 1)

    def inverse_factor(m):
        gram = gram_core[m, 0]
        for c in range(1, CORES):
            gram = gram + gram_core[m, c]
        copies = (lane_at < gram_lane) & (lax.rem(lane_at, rank) == row_at)
        work = jnp.where(copies, 1.0, gram)
        for k in range(rank):
            column = work[:, gram_lane + k:gram_lane + k + 1]
            row = work[k:k + 1]
            pivot = work[k:k + 1, gram_lane + k:gram_lane + k + 1]
            factor = jnp.where(row_at > k, column / pivot, 0.0)
            work = work - factor * row
        diagonal = jnp.sum(jnp.where(lane_at == row_at + gram_lane, work, 0.0), axis=1, keepdims=True)
        return work / jnp.sqrt(diagonal)

    def project(m):
        inverse = inverse_factor(m)
        high, middle, low = split3(inverse)
        group = lane_at // rank
        left = jnp.where((group == 2) | (group == 3), middle.astype(F32),
                         jnp.where(group == 5, low.astype(F32), high.astype(F32))).astype(BF16)
        left = left[:, 0:gram_lane]

        def body(t, total):
            value = jnp.concatenate([full[m, t * per_tile + j] for j in range(per_tile)], axis=1)
            xh, xm, xl = split3(value)
            q = nn_dot(left, jnp.concatenate([xh, xm, xh, xm, xl, xh], axis=0)).astype(BF16)
            q_low[m, t] = q
            span = pl.ds(pl.multiple_of(t * tile, tile), tile)
            return total + nn_dot(q, comp[m, span])
        total = lax.fori_loop(0, tiles, body, jnp.zeros((rank, cols), F32))
        right_all[m, dp] = total
        for k in range(1, n_dp):
            send(right_all.at[m, dp], right_all.at[m, dp], r_send.at[m, k], r_recv.at[m, dp],
                 (lax.rem(dp + k, n_dp), z))
        pltpu.make_async_copy(q_low.at[m], q_hbm.at[m], qstore_sem.at[m]).start()

    def right_finish(m):
        for k in range(1, n_dp):
            source = lax.rem(dp + k, n_dp)
            landed(right_all.at[m, source], r_send.at[m, k], r_recv.at[m, source])
        total = right_all[m, 0]
        for c in range(1, n_dp):
            total = total + right_all[m, c]
        right_low_ref[m] = (total * (1.0 / n_dp)).astype(BF16)

    pairs = [(core_finish, chip_start), (chip_finish, z_start), (z_finish, z_gather_start),
             (z_gather_finish, chip_gather_start), (chip_gather_finish, core_gather_start)]

    def advance(m, stage):
        for step in pairs[stage]:
            step(m)

    compensate(0, 0, tiles)
    core_start(0)
    compensate(1, 0, tiles // 2)
    advance(0, 0)
    compensate(1, tiles // 2, tiles)
    core_start(1)
    advance(0, 1)
    advance(1, 0)
    advance(0, 2)
    advance(1, 1)
    advance(0, 3)
    advance(1, 2)
    advance(0, 4)
    advance(1, 3)
    core_gather_finish(0)
    project(0)
    advance(1, 4)
    core_gather_finish(1)
    project(1)
    right_finish(0)
    right_finish(1)
    for copy in sent:
        copy.wait_send()
    for m in range(mats):
        pltpu.make_async_copy(q_low.at[m], q_hbm.at[m], qstore_sem.at[m]).wait()

        def end_store(t, carry, m=m):
            span = pl.ds(t * tile, tile)
            pltpu.make_async_copy(comp.at[m, span], comp_hbm.at[m, span], store_sem.at[m, t]).wait()
            return carry
        lax.fori_loop(0, tiles, end_store, 0)


def residue_kernel(comp_ref, q_ref, right_ref, feed_ref, update_ref):
    approx = lax.dot_general(q_ref[0, 0], right_ref[0], (((0,), (0,)), ((), ())),
                             preferred_element_type=F32)
    feed_ref[0, 0] = (comp_ref[0].astype(F32) - approx).astype(BF16)

    @pl.when(pl.program_id(1) == lax.axis_index("dp"))
    def _():
        update_ref[0] = approx.astype(BF16)


def shards(n_dp, n_mp, gradients, feedback, right_factor):
    _, mats, rows, cols = gradients.shape
    rank = right_factor.shape[2]
    tile = rows // n_dp
    tiles = rows // tile
    blocks = rows // LANES
    half_blocks = blocks // CORES
    chips = n_dp // CORES
    chip_blocks = half_blocks // chips
    z_blocks = chip_blocks // n_mp if chip_blocks % n_mp == 0 else chip_blocks
    dma = pltpu.SemaphoreType.DMA
    any_spec = pl.BlockSpec(memory_space=pl.ANY)
    vmem_spec = pl.BlockSpec(memory_space=pltpu.VMEM)
    comp, q_low, right_low = pl.pallas_call(
        functools.partial(reduce_kernel, n_dp, n_mp),
        out_shape=(
            jax.ShapeDtypeStruct((mats, rows, cols), BF16),
            jax.ShapeDtypeStruct((mats, tiles, rank, tile), BF16),
            jax.ShapeDtypeStruct((mats, rank, cols), BF16),
        ),
        in_specs=[any_spec, any_spec, vmem_spec],
        out_specs=(any_spec, any_spec, vmem_spec),
        scratch_shapes=[
            pltpu.VMEM((mats, rows, cols), BF16),
            pltpu.VMEM((mats, rows, cols), BF16),
            pltpu.VMEM((mats, blocks, rank, LANES), F32),
            pltpu.VMEM((mats, half_blocks, rank, LANES), F32),
            pltpu.VMEM((mats, half_blocks, rank, LANES), F32),
            pltpu.VMEM((mats, chips, chip_blocks, rank, LANES), F32),
            pltpu.VMEM((mats, chip_blocks, rank, LANES), F32),
            pltpu.VMEM((mats, n_mp, z_blocks, rank, LANES), F32),
            pltpu.VMEM((mats, blocks, rank, LANES), F32),
            pltpu.VMEM((mats, chips, rank, LANES), F32),
            pltpu.VMEM((mats, CORES, rank, LANES), F32),
            pltpu.VMEM((mats, tiles, rank, tile), BF16),
            pltpu.VMEM((mats, n_dp, rank, cols), F32),
            dma((2, mats, tiles)), dma((mats, tiles)), dma((mats,)),
            dma((mats,)), dma((mats,)), dma((mats, chips)), dma((mats, chips)),
            dma((mats, n_mp)), dma((mats, n_mp)),
            dma((mats, n_mp)), dma((mats, n_mp)), dma((mats, chips)), dma((mats, chips)),
            dma((mats,)), dma((mats,)),
            dma((mats, chips)), dma((mats, chips)), dma((mats,)), dma((mats,)),
            dma((mats, n_dp)), dma((mats, n_dp)),
        ],
        compiler_params=pltpu.CompilerParams(
            collective_id=0, has_side_effects=True, vmem_limit_bytes=48 * 1024 * 1024),
        name="reduce_factors",
    )(gradients, feedback, right_factor)
    return pl.pallas_call(
        residue_kernel,
        grid=(mats, tiles),
        out_shape=(
            jax.ShapeDtypeStruct((1, mats, rows, cols), BF16),
            jax.ShapeDtypeStruct((mats, tile, cols), BF16),
        ),
        in_specs=[
            pl.BlockSpec((1, tile, cols), lambda m, t: (m, t, 0)),
            pl.BlockSpec((1, 1, rank, tile), lambda m, t: (m, t, 0, 0)),
            pl.BlockSpec((1, rank, cols), lambda m, t: (m, 0, 0)),
        ],
        out_specs=(
            pl.BlockSpec((1, 1, tile, cols), lambda m, t: (0, m, t, 0)),
            pl.BlockSpec((1, tile, cols), lambda m, t: (m, 0, 0)),
        ),
        compiler_params=pltpu.CompilerParams(vmem_limit_bytes=24 * 1024 * 1024),
        name="subtract_approx",
    )(comp, q_low, right_low)


def solution(mesh):
    return jax.shard_map(
        functools.partial(shards, mesh.shape["dp"], mesh.shape["mp"]),
        mesh=mesh,
        in_specs=(P("dp", None, None, "mp"), P("dp", None, None, "mp"), P(None, "mp", None)),
        out_specs=(P("dp", None, None, "mp"), P(None, "dp", "mp")),
        check_vma=False,
    )
```

```python
import functools

import jax
import jax.numpy as jnp
from jax import lax
from jax.experimental import pallas as pl
from jax.experimental.pallas import tpu as pltpu
from jax.sharding import PartitionSpec as P

LANES = 128
CORES = 2
F32 = jnp.float32
BF16 = jnp.bfloat16


def split3(value):
    high = value.astype(BF16)
    rest = value - high.astype(F32)
    middle = rest.astype(BF16)
    low = (rest - middle.astype(F32)).astype(BF16)
    return high, middle, low


def nt_dot(left, right):
    return lax.dot_general(left, right, (((1,), (1,)), ((), ())), preferred_element_type=F32)


def nn_dot(left, right):
    return lax.dot_general(left, right, (((1,), (0,)), ((), ())), preferred_element_type=F32)


def reduce_kernel(
    n_dp, n_mp,
    grad_hbm, feed_hbm, right_ref,
    comp_hbm, q_hbm, right_low_ref,
    comp, feed, part, half, from_core, from_chip, plane, from_z, full,
    gram_chip, gram_core, q_low, right_all,
    load_sem, store_sem, qstore_sem,
    core_send, core_recv, chip_send, chip_recv, z_send, z_recv,
    zg_send, zg_recv, cg_send, cg_recv, kg_send, kg_recv,
    gc_send, gc_recv, gk_send, gk_recv, r_send, r_recv,
):
    mats, rows, cols = comp.shape
    rank = right_ref.shape[1]
    blocks = rows // LANES
    tile = q_low.shape[3]
    tiles = rows // tile
    per_tile = tile // LANES
    chips = n_dp // CORES
    half_blocks = blocks // CORES
    chip_blocks = half_blocks // chips
    z_split = chip_blocks % n_mp == 0
    z_blocks = chip_blocks // n_mp if z_split else chip_blocks

    dp = lax.axis_index("dp")
    z = lax.axis_index("mp")
    core = lax.rem(dp, CORES)
    chip = dp // CORES
    other = 1 - core
    twin = chip * CORES + other

    def loads(m, t):
        span = pl.ds(t * tile, tile)
        return (
            pltpu.make_async_copy(grad_hbm.at[0, m, span], comp.at[m, span], load_sem.at[0, m, t]),
            pltpu.make_async_copy(feed_hbm.at[0, m, span], feed.at[m, span], load_sem.at[1, m, t]),
        )

    for m in range(mats):
        def start_loads(t, carry, m=m):
            for copy in loads(m, t):
                copy.start()
            return carry
        lax.fori_loop(0, tiles, start_loads, 0)

    barrier = pltpu.get_barrier_semaphore()
    for k in range(1, n_dp):
        pl.semaphore_signal(barrier, inc=1, device_id=(lax.rem(dp + k, n_dp), z),
                            device_id_type=pl.DeviceIdType.MESH)
    for k in range(1, n_mp):
        pl.semaphore_signal(barrier, inc=1, device_id=(dp, lax.rem(z + k, n_mp)),
                            device_id_type=pl.DeviceIdType.MESH)
    pl.semaphore_wait(barrier, n_dp - 1 + n_mp - 1)

    sent = []

    def remote(src, dst, send_sem, recv_sem, device):
        return pltpu.make_async_remote_copy(
            src_ref=src, dst_ref=dst, send_sem=send_sem, recv_sem=recv_sem,
            device_id=device, device_id_type=pl.DeviceIdType.MESH)

    def send(*args):
        copy = remote(*args)
        copy.start()
        sent.append(copy)

    def landed(dst, send_sem, recv_sem):
        remote(dst, dst, send_sem, recv_sem, (twin, z)).wait_recv()

    def compensate(m, first, last):
        right_t = right_ref[m].astype(BF16)

        def body(t, carry):
            for copy in loads(m, t):
                copy.wait()
            span = pl.ds(pl.multiple_of(t * tile, tile), tile)
            value = (comp[m, span].astype(F32) + feed[m, span].astype(F32)).astype(BF16)
            comp[m, span] = value
            term = nt_dot(right_t, value)
            for j in range(per_tile):
                part[m, t * per_tile + j] = term[:, j * LANES:(j + 1) * LANES]
            pltpu.make_async_copy(comp.at[m, span], comp_hbm.at[m, span], store_sem.at[m, t]).start()
            return carry
        lax.fori_loop(first, last, body, 0)

    def core_start(m):
        send(part.at[m, pl.ds(other * half_blocks, half_blocks)], from_core.at[m],
             core_send.at[m], core_recv.at[m], (twin, z))

    def core_finish(m):
        landed(from_core.at[m], core_send.at[m], core_recv.at[m])
        half[m] = part[m, pl.ds(core * half_blocks, half_blocks)] + from_core[m]

    def chip_start(m):
        for k in range(1, chips):
            to = lax.rem(chip + k, chips)
            send(half.at[m, pl.ds(to * chip_blocks, chip_blocks)], from_chip.at[m, chip],
                 chip_send.at[m, k], chip_recv.at[m, chip], (to * CORES + core, z))

    def chip_finish(m):
        total = half[m, pl.ds(chip * chip_blocks, chip_blocks)]
        for k in range(1, chips):
            source = lax.rem(chip + k, chips)
            landed(from_chip.at[m, source], chip_send.at[m, k], chip_recv.at[m, source])
            total = total + from_chip[m, source]
        plane[m] = total

    def z_start(m):
        for k in range(1, n_mp):
            to = lax.rem(z + k, n_mp)
            first = to * z_blocks if z_split else 0
            send(plane.at[m, pl.ds(first, z_blocks)], from_z.at[m, z],
                 z_send.at[m, k], z_recv.at[m, z], (dp, to))

    base = core * half_blocks + chip * chip_blocks
    mine = pl.ds(base + (z * z_blocks if z_split else 0), z_blocks)

    def z_finish(m):
        total = plane[m, pl.ds(z * z_blocks if z_split else 0, z_blocks)]
        for k in range(1, n_mp):
            source = lax.rem(z + k, n_mp)
            landed(from_z.at[m, source], z_send.at[m, k], z_recv.at[m, source])
            total = total + from_z[m, source]
        full[m, mine] = total * (1.0 / n_dp)

    def z_gather_start(m):
        if z_split:
            for k in range(1, n_mp):
                send(full.at[m, mine], full.at[m, mine], zg_send.at[m, k], zg_recv.at[m, z],
                     (dp, lax.rem(z + k, n_mp)))

    def z_gather_finish(m):
        if z_split:
            for k in range(1, n_mp):
                source = lax.rem(z + k, n_mp)
                landed(full.at[m, pl.ds(base + source * z_blocks, z_blocks)],
                       zg_send.at[m, k], zg_recv.at[m, source])

    gram_lane = 6 * rank

    def chip_gather_start(m):
        own = pl.ds(base, chip_blocks)
        for k in range(1, chips):
            to = lax.rem(chip + k, chips)
            send(full.at[m, own], full.at[m, own], cg_send.at[m, k], cg_recv.at[m, chip],
                 (to * CORES + core, z))
        value = jnp.concatenate([full[m, base + j] for j in range(chip_blocks)], axis=1)
        terms = split3(value)
        tall = jnp.concatenate(terms, axis=0)
        pad = jnp.zeros((gram_lane, value.shape[1]), BF16)
        wide = sum(nt_dot(tall, jnp.concatenate([pad, term], axis=0)) for term in terms)
        gram = wide[0:rank] + wide[rank:2 * rank] + wide[2 * rank:3 * rank]
        gram_chip[m, chip] = jnp.zeros((rank, LANES), F32)
        gram_chip[m, chip, :, 0:gram_lane + rank] = gram
        for k in range(1, chips):
            to = lax.rem(chip + k, chips)
            send(gram_chip.at[m, chip], gram_chip.at[m, chip], gc_send.at[m, k],
                 gc_recv.at[m, chip], (to * CORES + core, z))

    def chip_gather_finish(m):
        for k in range(1, chips):
            source = lax.rem(chip + k, chips)
            landed(full.at[m, pl.ds(core * half_blocks + source * chip_blocks, chip_blocks)],
                   cg_send.at[m, k], cg_recv.at[m, source])
            landed(gram_chip.at[m, source], gc_send.at[m, k], gc_recv.at[m, source])

    def core_gather_start(m):
        own = pl.ds(core * half_blocks, half_blocks)
        send(full.at[m, own], full.at[m, own], kg_send.at[m], kg_recv.at[m], (twin, z))
        total = gram_chip[m, 0]
        for c in range(1, chips):
            total = total + gram_chip[m, c]
        gram_core[m, core] = total
        send(gram_core.at[m, core], gram_core.at[m, core], gk_send.at[m], gk_recv.at[m], (twin, z))

    def core_gather_finish(m):
        landed(gram_core.at[m, other], gk_send.at[m], gk_recv.at[m])
        landed(full.at[m, pl.ds(other * half_blocks, half_blocks)], kg_send.at[m], kg_recv.at[m])

    row_at = lax.broadcasted_iota(jnp.int32, (rank, LANES), 0)
    lane_at = lax.broadcasted_iota(jnp.int32, (rank, LANES), 1)

    def inverse_factor(m):
        gram = gram_core[m, 0]
        for c in range(1, CORES):
            gram = gram + gram_core[m, c]
        copies = (lane_at < gram_lane) & (lax.rem(lane_at, rank) == row_at)
        work = jnp.where(copies, 1.0, gram)
        for k in range(rank):
            column = work[:, gram_lane + k:gram_lane + k + 1]
            row = work[k:k + 1]
            pivot = work[k:k + 1, gram_lane + k:gram_lane + k + 1]
            factor = jnp.where(row_at > k, column / pivot, 0.0)
            work = work - factor * row
        diagonal = jnp.sum(jnp.where(lane_at == row_at + gram_lane, work, 0.0), axis=1, keepdims=True)
        return work / jnp.sqrt(diagonal)

    def project(m):
        inverse = inverse_factor(m)
        high, middle, low = split3(inverse)
        group = lane_at // rank
        left = jnp.where((group == 2) | (group == 3), middle.astype(F32),
                         jnp.where(group == 5, low.astype(F32), high.astype(F32))).astype(BF16)
        left = left[:, 0:gram_lane]

        def body(t, total):
            value = jnp.concatenate([full[m, t * per_tile + j] for j in range(per_tile)], axis=1)
            xh, xm, xl = split3(value)
            q = nn_dot(left, jnp.concatenate([xh, xm, xh, xm, xl, xh], axis=0)).astype(BF16)
            q_low[m, t] = q
            span = pl.ds(pl.multiple_of(t * tile, tile), tile)
            return total + nn_dot(q, comp[m, span])
        total = lax.fori_loop(0, tiles, body, jnp.zeros((rank, cols), F32), unroll=4)
        right_all[m, dp] = total
        for k in range(1, n_dp):
            send(right_all.at[m, dp], right_all.at[m, dp], r_send.at[m, k], r_recv.at[m, dp],
                 (lax.rem(dp + k, n_dp), z))
        pltpu.make_async_copy(q_low.at[m], q_hbm.at[m], qstore_sem.at[m]).start()

    def right_finish(m):
        for k in range(1, n_dp):
            source = lax.rem(dp + k, n_dp)
            landed(right_all.at[m, source], r_send.at[m, k], r_recv.at[m, source])
        total = right_all[m, 0]
        for c in range(1, n_dp):
            total = total + right_all[m, c]
        right_low_ref[m] = (total * (1.0 / n_dp)).astype(BF16)

    pairs = [(core_finish, chip_start), (chip_finish, z_start), (z_finish, z_gather_start),
             (z_gather_finish, chip_gather_start), (chip_gather_finish, core_gather_start)]

    def advance(m, stage):
        for step in pairs[stage]:
            step(m)

    compensate(0, 0, tiles)
    core_start(0)
    compensate(1, 0, tiles // 2)
    advance(0, 0)
    compensate(1, tiles // 2, tiles)
    core_start(1)
    advance(0, 1)
    advance(1, 0)
    advance(0, 2)
    advance(1, 1)
    advance(0, 3)
    advance(1, 2)
    advance(0, 4)
    advance(1, 3)
    core_gather_finish(0)
    project(0)
    advance(1, 4)
    core_gather_finish(1)
    project(1)
    right_finish(0)
    right_finish(1)
    for copy in sent:
        copy.wait_send()
    for m in range(mats):
        pltpu.make_async_copy(q_low.at[m], q_hbm.at[m], qstore_sem.at[m]).wait()

        def end_store(t, carry, m=m):
            span = pl.ds(t * tile, tile)
            pltpu.make_async_copy(comp.at[m, span], comp_hbm.at[m, span], store_sem.at[m, t]).wait()
            return carry
        lax.fori_loop(0, tiles, end_store, 0)


def residue_kernel(comp_hbm, q_hbm, right_ref, feed_hbm, update_hbm, comp, q_low, out, update,
                   load_sem, q_sem, store_sem, update_sem):
    mats, tiles, _, tile = q_low.shape
    dp = lax.axis_index("dp")

    def load(m, t):
        span = pl.ds(t * tile, tile)
        return pltpu.make_async_copy(comp_hbm.at[m, span], comp.at[m, span], load_sem.at[m, t])

    def store(m, t):
        span = pl.ds(t * tile, tile)
        return pltpu.make_async_copy(out.at[m, span], feed_hbm.at[0, m, span], store_sem.at[m, t])

    q_copies = [pltpu.make_async_copy(q_hbm.at[m], q_low.at[m], q_sem.at[m]) for m in range(mats)]
    for m in range(mats):
        q_copies[m].start()

        def start(t, carry, m=m):
            load(m, t).start()
            return carry
        lax.fori_loop(0, tiles, start, 0)
    for m in range(mats):
        q_copies[m].wait()
        right = right_ref[m]

        def body(t, carry, m=m, right=right):
            load(m, t).wait()
            span = pl.ds(pl.multiple_of(t * tile, tile), tile)
            approx = lax.dot_general(q_low[m, t], right, (((0,), (0,)), ((), ())),
                                     preferred_element_type=F32)
            out[m, span] = (comp[m, span].astype(F32) - approx).astype(BF16)
            store(m, t).start()

            @pl.when(t == dp)
            def _():
                update[m] = approx.astype(BF16)
            return carry
        lax.fori_loop(0, tiles, body, 0)
    update_copy = pltpu.make_async_copy(update, update_hbm, update_sem)
    update_copy.start()
    for m in range(mats):
        def finish(t, carry, m=m):
            store(m, t).wait()
            return carry
        lax.fori_loop(0, tiles, finish, 0)
    update_copy.wait()


def shards(n_dp, n_mp, gradients, feedback, right_factor):
    _, mats, rows, cols = gradients.shape
    rank = right_factor.shape[2]
    tile = rows // n_dp
    tiles = rows // tile
    blocks = rows // LANES
    half_blocks = blocks // CORES
    chips = n_dp // CORES
    chip_blocks = half_blocks // chips
    z_blocks = chip_blocks // n_mp if chip_blocks % n_mp == 0 else chip_blocks
    dma = pltpu.SemaphoreType.DMA
    any_spec = pl.BlockSpec(memory_space=pl.ANY)
    vmem_spec = pl.BlockSpec(memory_space=pltpu.VMEM)
    comp, q_low, right_low = pl.pallas_call(
        functools.partial(reduce_kernel, n_dp, n_mp),
        out_shape=(
            jax.ShapeDtypeStruct((mats, rows, cols), BF16),
            jax.ShapeDtypeStruct((mats, tiles, rank, tile), BF16),
            jax.ShapeDtypeStruct((mats, rank, cols), BF16),
        ),
        in_specs=[any_spec, any_spec, vmem_spec],
        out_specs=(any_spec, any_spec, vmem_spec),
        scratch_shapes=[
            pltpu.VMEM((mats, rows, cols), BF16),
            pltpu.VMEM((mats, rows, cols), BF16),
            pltpu.VMEM((mats, blocks, rank, LANES), F32),
            pltpu.VMEM((mats, half_blocks, rank, LANES), F32),
            pltpu.VMEM((mats, half_blocks, rank, LANES), F32),
            pltpu.VMEM((mats, chips, chip_blocks, rank, LANES), F32),
            pltpu.VMEM((mats, chip_blocks, rank, LANES), F32),
            pltpu.VMEM((mats, n_mp, z_blocks, rank, LANES), F32),
            pltpu.VMEM((mats, blocks, rank, LANES), F32),
            pltpu.VMEM((mats, chips, rank, LANES), F32),
            pltpu.VMEM((mats, CORES, rank, LANES), F32),
            pltpu.VMEM((mats, tiles, rank, tile), BF16),
            pltpu.VMEM((mats, n_dp, rank, cols), F32),
            dma((2, mats, tiles)), dma((mats, tiles)), dma((mats,)),
            dma((mats,)), dma((mats,)), dma((mats, chips)), dma((mats, chips)),
            dma((mats, n_mp)), dma((mats, n_mp)),
            dma((mats, n_mp)), dma((mats, n_mp)), dma((mats, chips)), dma((mats, chips)),
            dma((mats,)), dma((mats,)),
            dma((mats, chips)), dma((mats, chips)), dma((mats,)), dma((mats,)),
            dma((mats, n_dp)), dma((mats, n_dp)),
        ],
        compiler_params=pltpu.CompilerParams(
            collective_id=0, has_side_effects=True, vmem_limit_bytes=40 * 1024 * 1024),
        name="reduce_factors",
    )(gradients, feedback, jnp.swapaxes(right_factor, 1, 2))
    return pl.pallas_call(
        residue_kernel,
        out_shape=(
            jax.ShapeDtypeStruct((1, mats, rows, cols), BF16),
            jax.ShapeDtypeStruct((mats, tile, cols), BF16),
        ),
        in_specs=[any_spec, any_spec, vmem_spec],
        out_specs=(any_spec, any_spec),
        scratch_shapes=[
            pltpu.VMEM((mats, rows, cols), BF16),
            pltpu.VMEM((mats, tiles, rank, tile), BF16),
            pltpu.VMEM((mats, rows, cols), BF16),
            pltpu.VMEM((mats, tile, cols), BF16),
            dma((mats, tiles)), dma((mats,)), dma((mats, tiles)), dma,
        ],
        compiler_params=pltpu.CompilerParams(vmem_limit_bytes=24 * 1024 * 1024),
        name="subtract_approx",
    )(comp, q_low, right_low)


def solution(mesh):
    return jax.shard_map(
        functools.partial(shards, mesh.shape["dp"], mesh.shape["mp"]),
        mesh=mesh,
        in_specs=(P("dp", None, None, "mp"), P("dp", None, None, "mp"), P(None, "mp", None)),
        out_specs=(P("dp", None, None, "mp"), P(None, "dp", "mp")),
        check_vma=False,
    )
```

```python
import functools

import jax
import jax.numpy as jnp
from jax import lax
from jax.experimental import pallas as pl
from jax.experimental.pallas import tpu as pltpu
from jax.sharding import PartitionSpec as P

LANES = 128
CORES = 2
F32 = jnp.float32
BF16 = jnp.bfloat16


def split3(value):
    high = value.astype(BF16)
    rest = value - high.astype(F32)
    middle = rest.astype(BF16)
    low = (rest - middle.astype(F32)).astype(BF16)
    return high, middle, low


def nt_dot(left, right):
    return lax.dot_general(left, right, (((1,), (1,)), ((), ())), preferred_element_type=F32)


def nn_dot(left, right):
    return lax.dot_general(left, right, (((1,), (0,)), ((), ())), preferred_element_type=F32)


def tn_dot(left, right):
    return lax.dot_general(left, right, (((0,), (0,)), ((), ())), preferred_element_type=F32)


def reduce_kernel(
    n_dp, n_mp,
    grad_hbm, feed_hbm, right_ref,
    comp_hbm, q_hbm, right_low_ref,
    comp, feed, part, half, half_low, from_core, from_chip, plane, plane_low, from_z, full,
    gram_all, q_low, right_all,
    load_sem, store_sem, qstore_sem,
    core_send, core_recv, chip_send, chip_recv, z_send, z_recv,
    zg_send, zg_recv, cg_send, cg_recv, kg_send, kg_recv,
    gram_send, gram_recv, r_send, r_recv,
):
    mats, rows, cols = comp.shape
    rank = right_ref.shape[1]
    blocks = rows // LANES
    tile = q_low.shape[3]
    tiles = rows // tile
    per_tile = tile // LANES
    chips = n_dp // CORES
    half_blocks = blocks // CORES
    chip_blocks = half_blocks // chips
    z_split = chip_blocks % n_mp == 0
    z_blocks = chip_blocks // n_mp if z_split else chip_blocks

    dp = lax.axis_index("dp")
    z = lax.axis_index("mp")
    core = lax.rem(dp, CORES)
    chip = dp // CORES
    other = 1 - core
    twin = chip * CORES + other

    def loads(m, t):
        span = pl.ds(t * tile, tile)
        return (
            pltpu.make_async_copy(grad_hbm.at[0, m, span], comp.at[m, span], load_sem.at[0, m, t]),
            pltpu.make_async_copy(feed_hbm.at[0, m, span], feed.at[m, span], load_sem.at[1, m, t]),
        )

    for m in range(mats):
        def start_loads(t, carry, m=m):
            for copy in loads(m, t):
                copy.start()
            return carry
        lax.fori_loop(0, tiles, start_loads, 0)

    barrier = pltpu.get_barrier_semaphore()
    for k in range(1, n_dp):
        pl.semaphore_signal(barrier, inc=1, device_id=(lax.rem(dp + k, n_dp), z),
                            device_id_type=pl.DeviceIdType.MESH)
    for k in range(1, n_mp):
        pl.semaphore_signal(barrier, inc=1, device_id=(dp, lax.rem(z + k, n_mp)),
                            device_id_type=pl.DeviceIdType.MESH)
    pl.semaphore_wait(barrier, n_dp - 1 + n_mp - 1)

    sent = []

    def remote(src, dst, send_sem, recv_sem, device):
        return pltpu.make_async_remote_copy(
            src_ref=src, dst_ref=dst, send_sem=send_sem, recv_sem=recv_sem,
            device_id=device, device_id_type=pl.DeviceIdType.MESH)

    def send(*args):
        copy = remote(*args)
        copy.start()
        sent.append(copy)

    def landed(dst, send_sem, recv_sem):
        remote(dst, dst, send_sem, recv_sem, (twin, z)).wait_recv()

    def compensate(m, first, last):
        right_t = right_ref[m].astype(BF16)

        def body(t, carry):
            for copy in loads(m, t):
                copy.wait()
            span = pl.ds(pl.multiple_of(t * tile, tile), tile)
            value = (comp[m, span].astype(F32) + feed[m, span].astype(F32)).astype(BF16)
            comp[m, span] = value
            term = nt_dot(right_t, value)
            for j in range(per_tile):
                part[m, t * per_tile + j] = term[:, j * LANES:(j + 1) * LANES]
            pltpu.make_async_copy(comp.at[m, span], comp_hbm.at[m, span], store_sem.at[m, t]).start()
            return carry
        lax.fori_loop(first, last, body, 0)

    def core_start(m):
        send(part.at[m, pl.ds(other * half_blocks, half_blocks)], from_core.at[m],
             core_send.at[m], core_recv.at[m], (twin, z))

    def core_finish(m):
        landed(from_core.at[m], core_send.at[m], core_recv.at[m])
        total = part[m, pl.ds(core * half_blocks, half_blocks)] + from_core[m]
        half[m] = total
        half_low[m] = total.astype(BF16)

    def chip_start(m):
        for k in range(1, chips):
            to = lax.rem(chip + k, chips)
            send(half_low.at[m, pl.ds(to * chip_blocks, chip_blocks)], from_chip.at[m, chip],
                 chip_send.at[m, k], chip_recv.at[m, chip], (to * CORES + core, z))

    def chip_finish(m):
        total = half[m, pl.ds(chip * chip_blocks, chip_blocks)]
        for k in range(1, chips):
            source = lax.rem(chip + k, chips)
            landed(from_chip.at[m, source], chip_send.at[m, k], chip_recv.at[m, source])
            total = total + from_chip[m, source].astype(F32)
        plane[m] = total
        plane_low[m] = total.astype(BF16)

    def z_start(m):
        for k in range(1, n_mp):
            to = lax.rem(z + k, n_mp)
            first = to * z_blocks if z_split else 0
            send(plane_low.at[m, pl.ds(first, z_blocks)], from_z.at[m, z],
                 z_send.at[m, k], z_recv.at[m, z], (dp, to))

    base = core * half_blocks + chip * chip_blocks
    mine = pl.ds(base + (z * z_blocks if z_split else 0), z_blocks)

    def z_finish(m):
        total = plane[m, pl.ds(z * z_blocks if z_split else 0, z_blocks)]
        for k in range(1, n_mp):
            source = lax.rem(z + k, n_mp)
            landed(from_z.at[m, source], z_send.at[m, k], z_recv.at[m, source])
            total = total + from_z[m, source].astype(F32)
        full[m, mine] = total * (1.0 / n_dp)

    def z_gather_start(m):
        if z_split:
            for k in range(1, n_mp):
                send(full.at[m, mine], full.at[m, mine], zg_send.at[m, k], zg_recv.at[m, z],
                     (dp, lax.rem(z + k, n_mp)))

    def z_gather_finish(m):
        if z_split:
            for k in range(1, n_mp):
                source = lax.rem(z + k, n_mp)
                landed(full.at[m, pl.ds(base + source * z_blocks, z_blocks)],
                       zg_send.at[m, k], zg_recv.at[m, source])

    gram_lane = 6 * rank

    def chip_gather_start(m):
        value = jnp.concatenate([full[m, base + j] for j in range(chip_blocks)], axis=1)
        terms = split3(value)
        tall = jnp.concatenate(terms, axis=0)
        pad = jnp.zeros((gram_lane, value.shape[1]), BF16)
        wide = sum(nt_dot(tall, jnp.concatenate([pad, term], axis=0)) for term in terms)
        gram = wide[0:rank] + wide[rank:2 * rank] + wide[2 * rank:3 * rank]
        gram_all[m, dp] = jnp.zeros((rank, LANES), F32)
        gram_all[m, dp, :, 0:gram_lane + rank] = gram
        for k in range(1, n_dp):
            send(gram_all.at[m, dp], gram_all.at[m, dp], gram_send.at[m, k], gram_recv.at[m, dp],
                 (lax.rem(dp + k, n_dp), z))
        own = pl.ds(base, chip_blocks)
        for k in range(1, chips):
            to = lax.rem(chip + k, chips)
            send(full.at[m, own], full.at[m, own], cg_send.at[m, k], cg_recv.at[m, chip],
                 (to * CORES + core, z))

    def chip_gather_finish(m):
        for k in range(1, chips):
            source = lax.rem(chip + k, chips)
            landed(full.at[m, pl.ds(core * half_blocks + source * chip_blocks, chip_blocks)],
                   cg_send.at[m, k], cg_recv.at[m, source])

    def core_gather_start(m):
        own = pl.ds(core * half_blocks, half_blocks)
        send(full.at[m, own], full.at[m, own], kg_send.at[m], kg_recv.at[m], (twin, z))

    def core_gather_finish(m):
        landed(full.at[m, pl.ds(other * half_blocks, half_blocks)], kg_send.at[m], kg_recv.at[m])

    row_at = lax.broadcasted_iota(jnp.int32, (rank, LANES), 0)
    lane_at = lax.broadcasted_iota(jnp.int32, (rank, LANES), 1)

    def inverse_factor(m):
        for k in range(1, n_dp):
            source = lax.rem(dp + k, n_dp)
            landed(gram_all.at[m, source], gram_send.at[m, k], gram_recv.at[m, source])
        gram = gram_all[m, 0]
        for c in range(1, n_dp):
            gram = gram + gram_all[m, c]
        copies = (lane_at < gram_lane) & (lax.rem(lane_at, rank) == row_at)
        work = jnp.where(copies, 1.0, gram)
        for k in range(rank):
            column = work[:, gram_lane + k:gram_lane + k + 1]
            row = work[k:k + 1]
            pivot = work[k:k + 1, gram_lane + k:gram_lane + k + 1]
            factor = jnp.where(row_at > k, column / pivot, 0.0)
            work = work - factor * row
        diagonal = jnp.sum(jnp.where(lane_at == row_at + gram_lane, work, 0.0), axis=1, keepdims=True)
        return work / jnp.sqrt(diagonal)

    def project(m, inverse):
        high, middle, low = split3(inverse)
        group = lane_at // rank
        left = jnp.where((group == 2) | (group == 3), middle.astype(F32),
                         jnp.where(group == 5, low.astype(F32), high.astype(F32))).astype(BF16)
        left = left[:, 0:gram_lane]

        def body(t, total):
            value = jnp.concatenate([full[m, t * per_tile + j] for j in range(per_tile)], axis=1)
            xh, xm, xl = split3(value)
            q = nn_dot(left, jnp.concatenate([xh, xm, xh, xm, xl, xh], axis=0)).astype(BF16)
            q_low[m, t] = q
            span = pl.ds(pl.multiple_of(t * tile, tile), tile)
            return total + nn_dot(q, comp[m, span])
        total = lax.fori_loop(0, tiles, body, jnp.zeros((rank, cols), F32), unroll=4)
        right_all[m, dp] = total.astype(BF16)
        for k in range(1, n_dp):
            send(right_all.at[m, dp], right_all.at[m, dp], r_send.at[m, k], r_recv.at[m, dp],
                 (lax.rem(dp + k, n_dp), z))
        pltpu.make_async_copy(q_low.at[m], q_hbm.at[m], qstore_sem.at[m]).start()

    def right_finish(m):
        for k in range(1, n_dp):
            source = lax.rem(dp + k, n_dp)
            landed(right_all.at[m, source], r_send.at[m, k], r_recv.at[m, source])
        total = right_all[m, 0].astype(F32)
        for c in range(1, n_dp):
            total = total + right_all[m, c].astype(F32)
        right_low_ref[m] = (total * (1.0 / n_dp)).astype(BF16)

    pairs = [(core_finish, chip_start), (chip_finish, z_start), (z_finish, z_gather_start),
             (z_gather_finish, chip_gather_start), (chip_gather_finish, core_gather_start)]

    def advance(m, stage):
        for step in pairs[stage]:
            step(m)

    compensate(0, 0, tiles)
    core_start(0)
    compensate(1, 0, tiles // 2)
    advance(0, 0)
    compensate(1, tiles // 2, tiles)
    core_start(1)
    advance(0, 1)
    advance(1, 0)
    advance(0, 2)
    advance(1, 1)
    advance(0, 3)
    advance(1, 2)
    inverse_0 = inverse_factor(0)
    advance(0, 4)
    advance(1, 3)
    core_gather_finish(0)
    project(0, inverse_0)
    advance(1, 4)
    inverse_1 = inverse_factor(1)
    core_gather_finish(1)
    project(1, inverse_1)
    right_finish(0)
    right_finish(1)
    for copy in sent:
        copy.wait_send()
    for m in range(mats):
        pltpu.make_async_copy(q_low.at[m], q_hbm.at[m], qstore_sem.at[m]).wait()

        def end_store(t, carry, m=m):
            span = pl.ds(t * tile, tile)
            pltpu.make_async_copy(comp.at[m, span], comp_hbm.at[m, span], store_sem.at[m, t]).wait()
            return carry
        lax.fori_loop(0, tiles, end_store, 0)


def residue_kernel(comp_hbm, q_hbm, right_ref, feed_hbm, update_hbm, comp, q_low, out, update,
                   load_sem, q_sem, store_sem, update_sem):
    mats, tiles, _, tile = q_low.shape
    piece = min(tile, 2 * LANES)
    dp = lax.axis_index("dp")

    def load(m, t):
        span = pl.ds(t * tile, tile)
        return pltpu.make_async_copy(comp_hbm.at[m, span], comp.at[m, span], load_sem.at[m, t])

    def store(m, t):
        span = pl.ds(t * tile, tile)
        return pltpu.make_async_copy(out.at[m, span], feed_hbm.at[0, m, span], store_sem.at[m, t])

    q_copies = [pltpu.make_async_copy(q_hbm.at[m], q_low.at[m], q_sem.at[m]) for m in range(mats)]
    for m in range(mats):
        q_copies[m].start()

        def start(t, carry, m=m):
            load(m, t).start()
            return carry
        lax.fori_loop(0, tiles, start, 0)
    for m in range(mats):
        q_copies[m].wait()
        right = right_ref[m]

        def body(t, carry, m=m, right=right):
            load(m, t).wait()
            for r in range(0, tile, piece):
                approx = tn_dot(q_low[m, t, :, r:r + piece], right)
                rows = pl.ds(pl.multiple_of(t * tile + r, piece), piece)
                out[m, rows] = (comp[m, rows].astype(F32) - approx).astype(BF16)
            store(m, t).start()
            return carry
        lax.fori_loop(0, tiles, body, 0)
    for m in range(mats):
        for r in range(0, tile, piece):
            update[m, r:r + piece] = tn_dot(q_low[m, dp, :, r:r + piece], right_ref[m]).astype(BF16)
    update_copy = pltpu.make_async_copy(update, update_hbm, update_sem)
    update_copy.start()
    for m in range(mats):
        def finish(t, carry, m=m):
            store(m, t).wait()
            return carry
        lax.fori_loop(0, tiles, finish, 0)
    update_copy.wait()


def shards(n_dp, n_mp, gradients, feedback, right_factor):
    _, mats, rows, cols = gradients.shape
    rank = right_factor.shape[2]
    tile = rows // n_dp
    tiles = rows // tile
    blocks = rows // LANES
    half_blocks = blocks // CORES
    chips = n_dp // CORES
    chip_blocks = half_blocks // chips
    z_blocks = chip_blocks // n_mp if chip_blocks % n_mp == 0 else chip_blocks
    dma = pltpu.SemaphoreType.DMA
    any_spec = pl.BlockSpec(memory_space=pl.ANY)
    vmem_spec = pl.BlockSpec(memory_space=pltpu.VMEM)
    comp, q_low, right_low = pl.pallas_call(
        functools.partial(reduce_kernel, n_dp, n_mp),
        out_shape=(
            jax.ShapeDtypeStruct((mats, rows, cols), BF16),
            jax.ShapeDtypeStruct((mats, tiles, rank, tile), BF16),
            jax.ShapeDtypeStruct((mats, rank, cols), BF16),
        ),
        in_specs=[any_spec, any_spec, vmem_spec],
        out_specs=(any_spec, any_spec, vmem_spec),
        scratch_shapes=[
            pltpu.VMEM((mats, rows, cols), BF16),
            pltpu.VMEM((mats, rows, cols), BF16),
            pltpu.VMEM((mats, blocks, rank, LANES), F32),
            pltpu.VMEM((mats, half_blocks, rank, LANES), F32),
            pltpu.VMEM((mats, half_blocks, rank, LANES), BF16),
            pltpu.VMEM((mats, half_blocks, rank, LANES), F32),
            pltpu.VMEM((mats, chips, chip_blocks, rank, LANES), BF16),
            pltpu.VMEM((mats, chip_blocks, rank, LANES), F32),
            pltpu.VMEM((mats, chip_blocks, rank, LANES), BF16),
            pltpu.VMEM((mats, n_mp, z_blocks, rank, LANES), BF16),
            pltpu.VMEM((mats, blocks, rank, LANES), F32),
            pltpu.VMEM((mats, n_dp, rank, LANES), F32),
            pltpu.VMEM((mats, tiles, rank, tile), BF16),
            pltpu.VMEM((mats, n_dp, rank, cols), BF16),
            dma((2, mats, tiles)), dma((mats, tiles)), dma((mats,)),
            dma((mats,)), dma((mats,)), dma((mats, chips)), dma((mats, chips)),
            dma((mats, n_mp)), dma((mats, n_mp)),
            dma((mats, n_mp)), dma((mats, n_mp)), dma((mats, chips)), dma((mats, chips)),
            dma((mats,)), dma((mats,)),
            dma((mats, n_dp)), dma((mats, n_dp)), dma((mats, n_dp)), dma((mats, n_dp)),
        ],
        compiler_params=pltpu.CompilerParams(
            collective_id=0, has_side_effects=True, vmem_limit_bytes=40 * 1024 * 1024),
        name="reduce_factors",
    )(gradients, feedback, jnp.swapaxes(right_factor, 1, 2))
    return pl.pallas_call(
        residue_kernel,
        out_shape=(
            jax.ShapeDtypeStruct((1, mats, rows, cols), BF16),
            jax.ShapeDtypeStruct((mats, tile, cols), BF16),
        ),
        in_specs=[any_spec, any_spec, vmem_spec],
        out_specs=(any_spec, any_spec),
        scratch_shapes=[
            pltpu.VMEM((mats, rows, cols), BF16),
            pltpu.VMEM((mats, tiles, rank, tile), BF16),
            pltpu.VMEM((mats, rows, cols), BF16),
            pltpu.VMEM((mats, tile, cols), BF16),
            dma((mats, tiles)), dma((mats,)), dma((mats, tiles)), dma,
        ],
        compiler_params=pltpu.CompilerParams(vmem_limit_bytes=24 * 1024 * 1024),
        name="subtract_approx",
    )(comp, q_low, right_low)


def solution(mesh):
    return jax.shard_map(
        functools.partial(shards, mesh.shape["dp"], mesh.shape["mp"]),
        mesh=mesh,
        in_specs=(P("dp", None, None, "mp"), P("dp", None, None, "mp"), P(None, "mp", None)),
        out_specs=(P("dp", None, None, "mp"), P(None, "dp", "mp")),
        check_vma=False,
    )
```

```python
import functools

import jax
import jax.numpy as jnp
from jax import lax
from jax.experimental import pallas as pl
from jax.experimental.pallas import tpu as pltpu
from jax.sharding import PartitionSpec as P

LANES = 128
CORES = 2
F32 = jnp.float32
BF16 = jnp.bfloat16


def split3(value):
    high = value.astype(BF16)
    rest = value - high.astype(F32)
    middle = rest.astype(BF16)
    low = (rest - middle.astype(F32)).astype(BF16)
    return high, middle, low


def nt_dot(left, right):
    return lax.dot_general(left, right, (((1,), (1,)), ((), ())), preferred_element_type=F32)


def nn_dot(left, right):
    return lax.dot_general(left, right, (((1,), (0,)), ((), ())), preferred_element_type=F32)


def tn_dot(left, right):
    return lax.dot_general(left, right, (((0,), (0,)), ((), ())), preferred_element_type=F32)


def reduce_kernel(
    n_dp, n_mp,
    grad_hbm, feed_hbm, right_ref,
    comp, q_low, right_low_ref,
    feed, part, half, half_low, from_core, from_chip, plane, plane_low, from_z, full,
    gram_all, right_all,
    load_sem,
    core_send, core_recv, chip_send, chip_recv, z_send, z_recv,
    zg_send, zg_recv, cg_send, cg_recv, kg_send, kg_recv,
    gram_send, gram_recv, r_send, r_recv,
):
    mats, rows, cols = comp.shape
    rank = right_ref.shape[1]
    blocks = rows // LANES
    tile = q_low.shape[3]
    tiles = rows // tile
    per_tile = tile // LANES
    chips = n_dp // CORES
    half_blocks = blocks // CORES
    chip_blocks = half_blocks // chips
    z_split = chip_blocks % n_mp == 0
    z_blocks = chip_blocks // n_mp if z_split else chip_blocks

    dp = lax.axis_index("dp")
    z = lax.axis_index("mp")
    core = lax.rem(dp, CORES)
    chip = dp // CORES
    other = 1 - core
    twin = chip * CORES + other

    def loads(m, t):
        span = pl.ds(t * tile, tile)
        return (
            pltpu.make_async_copy(grad_hbm.at[0, m, span], comp.at[m, span], load_sem.at[0, m, t]),
            pltpu.make_async_copy(feed_hbm.at[0, m, span], feed.at[m, span], load_sem.at[1, m, t]),
        )

    for m in range(mats):
        def start_loads(t, carry, m=m):
            for copy in loads(m, t):
                copy.start()
            return carry
        lax.fori_loop(0, tiles, start_loads, 0)

    barrier = pltpu.get_barrier_semaphore()
    for k in range(1, n_dp):
        pl.semaphore_signal(barrier, inc=1, device_id=(lax.rem(dp + k, n_dp), z),
                            device_id_type=pl.DeviceIdType.MESH)
    for k in range(1, n_mp):
        pl.semaphore_signal(barrier, inc=1, device_id=(dp, lax.rem(z + k, n_mp)),
                            device_id_type=pl.DeviceIdType.MESH)
    pl.semaphore_wait(barrier, n_dp - 1 + n_mp - 1)

    sent = []

    def remote(src, dst, send_sem, recv_sem, device):
        return pltpu.make_async_remote_copy(
            src_ref=src, dst_ref=dst, send_sem=send_sem, recv_sem=recv_sem,
            device_id=device, device_id_type=pl.DeviceIdType.MESH)

    def send(*args):
        copy = remote(*args)
        copy.start()
        sent.append(copy)

    def landed(dst, send_sem, recv_sem):
        remote(dst, dst, send_sem, recv_sem, (twin, z)).wait_recv()

    def compensate(m, first, last):
        right_t = right_ref[m].astype(BF16)

        def body(t, carry):
            for copy in loads(m, t):
                copy.wait()
            span = pl.ds(pl.multiple_of(t * tile, tile), tile)
            value = (comp[m, span].astype(F32) + feed[m, span].astype(F32)).astype(BF16)
            comp[m, span] = value
            term = nt_dot(right_t, value)
            for j in range(per_tile):
                part[m, t * per_tile + j] = term[:, j * LANES:(j + 1) * LANES]
            return carry
        lax.fori_loop(first, last, body, 0)

    def core_start(m):
        send(part.at[m, pl.ds(other * half_blocks, half_blocks)], from_core.at[m],
             core_send.at[m], core_recv.at[m], (twin, z))

    def core_finish(m):
        landed(from_core.at[m], core_send.at[m], core_recv.at[m])
        total = part[m, pl.ds(core * half_blocks, half_blocks)] + from_core[m]
        half[m] = total
        half_low[m] = total.astype(BF16)

    def chip_start(m):
        for k in range(1, chips):
            to = lax.rem(chip + k, chips)
            send(half_low.at[m, pl.ds(to * chip_blocks, chip_blocks)], from_chip.at[m, chip],
                 chip_send.at[m, k], chip_recv.at[m, chip], (to * CORES + core, z))

    def chip_finish(m):
        total = half[m, pl.ds(chip * chip_blocks, chip_blocks)]
        for k in range(1, chips):
            source = lax.rem(chip + k, chips)
            landed(from_chip.at[m, source], chip_send.at[m, k], chip_recv.at[m, source])
            total = total + from_chip[m, source].astype(F32)
        plane[m] = total
        plane_low[m] = total.astype(BF16)

    def z_start(m):
        for k in range(1, n_mp):
            to = lax.rem(z + k, n_mp)
            first = to * z_blocks if z_split else 0
            send(plane_low.at[m, pl.ds(first, z_blocks)], from_z.at[m, z],
                 z_send.at[m, k], z_recv.at[m, z], (dp, to))

    base = core * half_blocks + chip * chip_blocks
    mine = pl.ds(base + (z * z_blocks if z_split else 0), z_blocks)

    def z_finish(m):
        total = plane[m, pl.ds(z * z_blocks if z_split else 0, z_blocks)]
        for k in range(1, n_mp):
            source = lax.rem(z + k, n_mp)
            landed(from_z.at[m, source], z_send.at[m, k], z_recv.at[m, source])
            total = total + from_z[m, source].astype(F32)
        full[m, mine] = total * (1.0 / n_dp)

    def z_gather_start(m):
        if z_split:
            for k in range(1, n_mp):
                send(full.at[m, mine], full.at[m, mine], zg_send.at[m, k], zg_recv.at[m, z],
                     (dp, lax.rem(z + k, n_mp)))

    def z_gather_finish(m):
        if z_split:
            for k in range(1, n_mp):
                source = lax.rem(z + k, n_mp)
                landed(full.at[m, pl.ds(base + source * z_blocks, z_blocks)],
                       zg_send.at[m, k], zg_recv.at[m, source])

    gram_lane = 6 * rank

    def chip_gather_start(m):
        value = jnp.concatenate([full[m, base + j] for j in range(chip_blocks)], axis=1)
        terms = split3(value)
        tall = jnp.concatenate(terms, axis=0)
        pad = jnp.zeros((gram_lane, value.shape[1]), BF16)
        wide = sum(nt_dot(tall, jnp.concatenate([pad, term], axis=0)) for term in terms)
        gram = wide[0:rank] + wide[rank:2 * rank] + wide[2 * rank:3 * rank]
        gram_all[m, dp] = jnp.zeros((rank, LANES), F32)
        gram_all[m, dp, :, 0:gram_lane + rank] = gram
        for k in range(1, n_dp):
            send(gram_all.at[m, dp], gram_all.at[m, dp], gram_send.at[m, k], gram_recv.at[m, dp],
                 (lax.rem(dp + k, n_dp), z))
        own = pl.ds(base, chip_blocks)
        for k in range(1, chips):
            to = lax.rem(chip + k, chips)
            send(full.at[m, own], full.at[m, own], cg_send.at[m, k], cg_recv.at[m, chip],
                 (to * CORES + core, z))

    def chip_gather_finish(m):
        for k in range(1, chips):
            source = lax.rem(chip + k, chips)
            landed(full.at[m, pl.ds(core * half_blocks + source * chip_blocks, chip_blocks)],
                   cg_send.at[m, k], cg_recv.at[m, source])

    def core_gather_start(m):
        own = pl.ds(core * half_blocks, half_blocks)
        send(full.at[m, own], full.at[m, own], kg_send.at[m], kg_recv.at[m], (twin, z))

    def core_gather_finish(m):
        landed(full.at[m, pl.ds(other * half_blocks, half_blocks)], kg_send.at[m], kg_recv.at[m])

    row_at = lax.broadcasted_iota(jnp.int32, (rank, LANES), 0)
    lane_at = lax.broadcasted_iota(jnp.int32, (rank, LANES), 1)

    def inverse_factor(m):
        for k in range(1, n_dp):
            source = lax.rem(dp + k, n_dp)
            landed(gram_all.at[m, source], gram_send.at[m, k], gram_recv.at[m, source])
        gram = gram_all[m, 0]
        for c in range(1, n_dp):
            gram = gram + gram_all[m, c]
        copies = (lane_at < gram_lane) & (lax.rem(lane_at, rank) == row_at)
        work = jnp.where(copies, 1.0, gram)
        for k in range(rank):
            column = work[:, gram_lane + k:gram_lane + k + 1]
            row = work[k:k + 1]
            pivot = work[k:k + 1, gram_lane + k:gram_lane + k + 1]
            factor = jnp.where(row_at > k, column / pivot, 0.0)
            work = work - factor * row
        diagonal = jnp.sum(jnp.where(lane_at == row_at + gram_lane, work, 0.0), axis=1, keepdims=True)
        return work / jnp.sqrt(diagonal)

    def project(m, inverse):
        high, middle, low = split3(inverse)
        group = lane_at // rank
        left = jnp.where((group == 2) | (group == 3), middle.astype(F32),
                         jnp.where(group == 5, low.astype(F32), high.astype(F32))).astype(BF16)
        left = left[:, 0:gram_lane]

        def body(t, total):
            value = jnp.concatenate([full[m, t * per_tile + j] for j in range(per_tile)], axis=1)
            xh, xm, xl = split3(value)
            q = nn_dot(left, jnp.concatenate([xh, xm, xh, xm, xl, xh], axis=0)).astype(BF16)
            q_low[m, t] = q
            span = pl.ds(pl.multiple_of(t * tile, tile), tile)
            return total + nn_dot(q, comp[m, span])
        total = lax.fori_loop(0, tiles, body, jnp.zeros((rank, cols), F32), unroll=4)
        right_all[m, dp] = total.astype(BF16)
        for k in range(1, n_dp):
            send(right_all.at[m, dp], right_all.at[m, dp], r_send.at[m, k], r_recv.at[m, dp],
                 (lax.rem(dp + k, n_dp), z))

    def right_finish(m):
        for k in range(1, n_dp):
            source = lax.rem(dp + k, n_dp)
            landed(right_all.at[m, source], r_send.at[m, k], r_recv.at[m, source])
        total = right_all[m, 0].astype(F32)
        for c in range(1, n_dp):
            total = total + right_all[m, c].astype(F32)
        right_low_ref[m] = (total * (1.0 / n_dp)).astype(BF16)

    pairs = [(core_finish, chip_start), (chip_finish, z_start), (z_finish, z_gather_start),
             (z_gather_finish, chip_gather_start), (chip_gather_finish, core_gather_start)]

    def advance(m, stage):
        for step in pairs[stage]:
            step(m)

    compensate(0, 0, tiles)
    core_start(0)
    compensate(1, 0, tiles // 2)
    advance(0, 0)
    compensate(1, tiles // 2, tiles)
    core_start(1)
    advance(0, 1)
    advance(1, 0)
    advance(0, 2)
    advance(1, 1)
    advance(0, 3)
    advance(1, 2)
    inverse_0 = inverse_factor(0)
    advance(0, 4)
    advance(1, 3)
    core_gather_finish(0)
    project(0, inverse_0)
    advance(1, 4)
    inverse_1 = inverse_factor(1)
    core_gather_finish(1)
    project(1, inverse_1)
    right_finish(0)
    right_finish(1)
    for copy in sent:
        copy.wait_send()


def residue_kernel(comp, q_low, right_ref, feed_hbm, update_hbm, out, update, store_sem, update_sem):
    mats, tiles, _, tile = q_low.shape
    piece = min(tile, 2 * LANES)
    dp = lax.axis_index("dp")

    def store(m, t):
        span = pl.ds(t * tile, tile)
        return pltpu.make_async_copy(out.at[m, span], feed_hbm.at[0, m, span], store_sem.at[m, t])

    for m in range(mats):
        right = right_ref[m]

        def body(t, carry, m=m, right=right):
            for r in range(0, tile, piece):
                approx = tn_dot(q_low[m, t, :, r:r + piece], right)
                rows = pl.ds(pl.multiple_of(t * tile + r, piece), piece)
                out[m, rows] = (comp[m, rows].astype(F32) - approx).astype(BF16)
            store(m, t).start()
            return carry
        lax.fori_loop(0, tiles, body, 0)
    for m in range(mats):
        for r in range(0, tile, piece):
            update[m, r:r + piece] = tn_dot(q_low[m, dp, :, r:r + piece], right_ref[m]).astype(BF16)
    update_copy = pltpu.make_async_copy(update, update_hbm, update_sem)
    update_copy.start()
    for m in range(mats):
        def finish(t, carry, m=m):
            store(m, t).wait()
            return carry
        lax.fori_loop(0, tiles, finish, 0)
    update_copy.wait()


def shards(n_dp, n_mp, gradients, feedback, right_factor):
    _, mats, rows, cols = gradients.shape
    rank = right_factor.shape[2]
    tile = rows // n_dp
    tiles = rows // tile
    blocks = rows // LANES
    half_blocks = blocks // CORES
    chips = n_dp // CORES
    chip_blocks = half_blocks // chips
    z_blocks = chip_blocks // n_mp if chip_blocks % n_mp == 0 else chip_blocks
    dma = pltpu.SemaphoreType.DMA
    any_spec = pl.BlockSpec(memory_space=pl.ANY)
    vmem_spec = pl.BlockSpec(memory_space=pltpu.VMEM)
    comp, q_low, right_low = pl.pallas_call(
        functools.partial(reduce_kernel, n_dp, n_mp),
        out_shape=(
            jax.ShapeDtypeStruct((mats, rows, cols), BF16),
            jax.ShapeDtypeStruct((mats, tiles, rank, tile), BF16),
            jax.ShapeDtypeStruct((mats, rank, cols), BF16),
        ),
        in_specs=[any_spec, any_spec, vmem_spec],
        out_specs=(vmem_spec, vmem_spec, vmem_spec),
        scratch_shapes=[
            pltpu.VMEM((mats, rows, cols), BF16),
            pltpu.VMEM((mats, blocks, rank, LANES), F32),
            pltpu.VMEM((mats, half_blocks, rank, LANES), F32),
            pltpu.VMEM((mats, half_blocks, rank, LANES), BF16),
            pltpu.VMEM((mats, half_blocks, rank, LANES), F32),
            pltpu.VMEM((mats, chips, chip_blocks, rank, LANES), BF16),
            pltpu.VMEM((mats, chip_blocks, rank, LANES), F32),
            pltpu.VMEM((mats, chip_blocks, rank, LANES), BF16),
            pltpu.VMEM((mats, n_mp, z_blocks, rank, LANES), BF16),
            pltpu.VMEM((mats, blocks, rank, LANES), F32),
            pltpu.VMEM((mats, n_dp, rank, LANES), F32),
            pltpu.VMEM((mats, n_dp, rank, cols), BF16),
            dma((2, mats, tiles)),
            dma((mats,)), dma((mats,)), dma((mats, chips)), dma((mats, chips)),
            dma((mats, n_mp)), dma((mats, n_mp)),
            dma((mats, n_mp)), dma((mats, n_mp)), dma((mats, chips)), dma((mats, chips)),
            dma((mats,)), dma((mats,)),
            dma((mats, n_dp)), dma((mats, n_dp)), dma((mats, n_dp)), dma((mats, n_dp)),
        ],
        compiler_params=pltpu.CompilerParams(
            collective_id=0, has_side_effects=True, vmem_limit_bytes=44 * 1024 * 1024),
        name="reduce_factors",
    )(gradients, feedback, jnp.swapaxes(right_factor, 1, 2))
    return pl.pallas_call(
        residue_kernel,
        out_shape=(
            jax.ShapeDtypeStruct((1, mats, rows, cols), BF16),
            jax.ShapeDtypeStruct((mats, tile, cols), BF16),
        ),
        in_specs=[vmem_spec, vmem_spec, vmem_spec],
        out_specs=(any_spec, any_spec),
        scratch_shapes=[
            pltpu.VMEM((mats, rows, cols), BF16),
            pltpu.VMEM((mats, tile, cols), BF16),
            dma((mats, tiles)), dma,
        ],
        compiler_params=pltpu.CompilerParams(vmem_limit_bytes=24 * 1024 * 1024),
        name="subtract_approx",
    )(comp, q_low, right_low)


def solution(mesh):
    return jax.shard_map(
        functools.partial(shards, mesh.shape["dp"], mesh.shape["mp"]),
        mesh=mesh,
        in_specs=(P("dp", None, None, "mp"), P("dp", None, None, "mp"), P(None, "mp", None)),
        out_specs=(P("dp", None, None, "mp"), P(None, "dp", "mp")),
        check_vma=False,
    )
```

```python
import functools

import jax
import jax.numpy as jnp
from jax import lax
from jax.experimental import pallas as pl
from jax.experimental.pallas import tpu as pltpu
from jax.sharding import PartitionSpec as P

LANES = 128
CORES = 2
F32 = jnp.float32
BF16 = jnp.bfloat16


def split3(value):
    high = value.astype(BF16)
    rest = value - high.astype(F32)
    middle = rest.astype(BF16)
    low = (rest - middle.astype(F32)).astype(BF16)
    return high, middle, low


def nt_dot(left, right):
    return lax.dot_general(left, right, (((1,), (1,)), ((), ())), preferred_element_type=F32)


def nn_dot(left, right):
    return lax.dot_general(left, right, (((1,), (0,)), ((), ())), preferred_element_type=F32)


def tn_dot(left, right):
    return lax.dot_general(left, right, (((0,), (0,)), ((), ())), preferred_element_type=F32)


def reduce_kernel(
    n_dp, n_mp,
    grad_hbm, feed_hbm, right_ref,
    comp, q_low, right_low_ref,
    feed, part, half, half_low, from_core, from_chip, plane, plane_low, from_z, full,
    gram_all, right_all,
    load_sem,
    core_send, core_recv, chip_send, chip_recv, z_send, z_recv,
    zg_send, zg_recv, cg_send, cg_recv, kg_send, kg_recv,
    gram_send, gram_recv, r_send, r_recv,
):
    mats, rows, cols = comp.shape
    rank = right_ref.shape[1]
    blocks = rows // LANES
    tile = q_low.shape[3]
    tiles = rows // tile
    per_tile = tile // LANES
    chips = n_dp // CORES
    half_blocks = blocks // CORES
    chip_blocks = half_blocks // chips
    z_split = chip_blocks % n_mp == 0
    z_blocks = chip_blocks // n_mp if z_split else chip_blocks

    dp = lax.axis_index("dp")
    z = lax.axis_index("mp")
    core = lax.rem(dp, CORES)
    chip = dp // CORES
    other = 1 - core
    twin = chip * CORES + other

    def loads(m, t):
        span = pl.ds(t * tile, tile)
        return (
            pltpu.make_async_copy(grad_hbm.at[0, m, span], comp.at[m, span], load_sem.at[0, m, t]),
            pltpu.make_async_copy(feed_hbm.at[0, m, span], feed.at[m, span], load_sem.at[1, m, t]),
        )

    for m in range(mats):
        def start_loads(t, carry, m=m):
            for copy in loads(m, t):
                copy.start()
            return carry
        lax.fori_loop(0, tiles, start_loads, 0)

    barrier = pltpu.get_barrier_semaphore()
    for k in range(1, n_dp):
        pl.semaphore_signal(barrier, inc=1, device_id=(lax.rem(dp + k, n_dp), z),
                            device_id_type=pl.DeviceIdType.MESH)
    for k in range(1, n_mp):
        pl.semaphore_signal(barrier, inc=1, device_id=(dp, lax.rem(z + k, n_mp)),
                            device_id_type=pl.DeviceIdType.MESH)
    pl.semaphore_wait(barrier, n_dp - 1 + n_mp - 1)

    sent = []

    def remote(src, dst, send_sem, recv_sem, device):
        return pltpu.make_async_remote_copy(
            src_ref=src, dst_ref=dst, send_sem=send_sem, recv_sem=recv_sem,
            device_id=device, device_id_type=pl.DeviceIdType.MESH)

    def send(*args):
        copy = remote(*args)
        copy.start()
        sent.append(copy)

    def landed(dst, send_sem, recv_sem):
        remote(dst, dst, send_sem, recv_sem, (twin, z)).wait_recv()

    def compensate(m, first, last):
        right_t = right_ref[m].astype(BF16)

        def body(t, carry):
            for copy in loads(m, t):
                copy.wait()
            span = pl.ds(pl.multiple_of(t * tile, tile), tile)
            value = (comp[m, span].astype(F32) + feed[m, span].astype(F32)).astype(BF16)
            comp[m, span] = value
            term = nt_dot(right_t, value)
            for j in range(per_tile):
                part[m, t * per_tile + j] = term[:, j * LANES:(j + 1) * LANES]
            return carry
        lax.fori_loop(first, last, body, 0)

    def core_start(m):
        send(part.at[m, pl.ds(other * half_blocks, half_blocks)], from_core.at[m],
             core_send.at[m], core_recv.at[m], (twin, z))

    def core_finish(m):
        landed(from_core.at[m], core_send.at[m], core_recv.at[m])
        total = part[m, pl.ds(core * half_blocks, half_blocks)] + from_core[m]
        half[m] = total
        half_low[m] = total.astype(BF16)

    def chip_start(m):
        for k in range(1, chips):
            to = lax.rem(chip + k, chips)
            send(half_low.at[m, pl.ds(to * chip_blocks, chip_blocks)], from_chip.at[m, chip],
                 chip_send.at[m, k], chip_recv.at[m, chip], (to * CORES + core, z))

    def chip_finish(m):
        total = half[m, pl.ds(chip * chip_blocks, chip_blocks)]
        for k in range(1, chips):
            source = lax.rem(chip + k, chips)
            landed(from_chip.at[m, source], chip_send.at[m, k], chip_recv.at[m, source])
            total = total + from_chip[m, source].astype(F32)
        plane[m] = total
        plane_low[m] = total.astype(BF16)

    def z_start(m):
        for k in range(1, n_mp):
            to = lax.rem(z + k, n_mp)
            first = to * z_blocks if z_split else 0
            send(plane_low.at[m, pl.ds(first, z_blocks)], from_z.at[m, z],
                 z_send.at[m, k], z_recv.at[m, z], (dp, to))

    base = core * half_blocks + chip * chip_blocks
    mine = pl.ds(base + (z * z_blocks if z_split else 0), z_blocks)

    def z_finish(m):
        total = plane[m, pl.ds(z * z_blocks if z_split else 0, z_blocks)]
        for k in range(1, n_mp):
            source = lax.rem(z + k, n_mp)
            landed(from_z.at[m, source], z_send.at[m, k], z_recv.at[m, source])
            total = total + from_z[m, source].astype(F32)
        full[m, mine] = total * (1.0 / n_dp)

    def z_gather_start(m):
        if z_split:
            for k in range(1, n_mp):
                send(full.at[m, mine], full.at[m, mine], zg_send.at[m, k], zg_recv.at[m, z],
                     (dp, lax.rem(z + k, n_mp)))

    def z_gather_finish(m):
        if z_split:
            for k in range(1, n_mp):
                source = lax.rem(z + k, n_mp)
                landed(full.at[m, pl.ds(base + source * z_blocks, z_blocks)],
                       zg_send.at[m, k], zg_recv.at[m, source])

    gram_lane = 6 * rank

    def chip_gather_start(m):
        value = jnp.concatenate([full[m, base + j] for j in range(chip_blocks)], axis=1)
        terms = split3(value)
        tall = jnp.concatenate(terms, axis=0)
        pad = jnp.zeros((gram_lane, value.shape[1]), BF16)
        wide = sum(nt_dot(tall, jnp.concatenate([pad, term], axis=0)) for term in terms)
        gram = wide[0:rank] + wide[rank:2 * rank] + wide[2 * rank:3 * rank]
        gram_all[m, dp] = jnp.zeros((rank, LANES), F32)
        gram_all[m, dp, :, 0:gram_lane + rank] = gram
        for k in range(1, n_dp):
            send(gram_all.at[m, dp], gram_all.at[m, dp], gram_send.at[m, k], gram_recv.at[m, dp],
                 (lax.rem(dp + k, n_dp), z))
        own = pl.ds(base, chip_blocks)
        for k in range(1, chips):
            to = lax.rem(chip + k, chips)
            send(full.at[m, own], full.at[m, own], cg_send.at[m, k], cg_recv.at[m, chip],
                 (to * CORES + core, z))

    def chip_gather_finish(m):
        for k in range(1, chips):
            source = lax.rem(chip + k, chips)
            landed(full.at[m, pl.ds(core * half_blocks + source * chip_blocks, chip_blocks)],
                   cg_send.at[m, k], cg_recv.at[m, source])

    def core_gather_start(m):
        own = pl.ds(core * half_blocks, half_blocks)
        send(full.at[m, own], full.at[m, own], kg_send.at[m], kg_recv.at[m], (twin, z))

    def core_gather_finish(m):
        landed(full.at[m, pl.ds(other * half_blocks, half_blocks)], kg_send.at[m], kg_recv.at[m])

    row_at = lax.broadcasted_iota(jnp.int32, (rank, LANES), 0)
    lane_at = lax.broadcasted_iota(jnp.int32, (rank, LANES), 1)

    def inverse_factor(m):
        for k in range(1, n_dp):
            source = lax.rem(dp + k, n_dp)
            landed(gram_all.at[m, source], gram_send.at[m, k], gram_recv.at[m, source])
        gram = gram_all[m, 0]
        for c in range(1, n_dp):
            gram = gram + gram_all[m, c]
        copies = (lane_at < gram_lane) & (lax.rem(lane_at, rank) == row_at)
        work = jnp.where(copies, 1.0, gram)
        for k in range(rank):
            column = work[:, gram_lane + k:gram_lane + k + 1]
            row = work[k:k + 1]
            pivot = work[k:k + 1, gram_lane + k:gram_lane + k + 1]
            factor = jnp.where(row_at > k, column / pivot, 0.0)
            work = work - factor * row
        diagonal = jnp.sum(jnp.where(lane_at == row_at + gram_lane, work, 0.0), axis=1, keepdims=True)
        return work / jnp.sqrt(diagonal)

    def project(m, inverse):
        high, middle, low = split3(inverse)
        group = lane_at // rank
        left = jnp.where((group == 2) | (group == 3), middle.astype(F32),
                         jnp.where(group == 5, low.astype(F32), high.astype(F32))).astype(BF16)
        left = left[:, 0:gram_lane]

        def body(t, total):
            value = jnp.concatenate([full[m, t * per_tile + j] for j in range(per_tile)], axis=1)
            xh, xm, xl = split3(value)
            q = nn_dot(left, jnp.concatenate([xh, xm, xh, xm, xl, xh], axis=0)).astype(BF16)
            q_low[m, t] = q
            span = pl.ds(pl.multiple_of(t * tile, tile), tile)
            return total + nn_dot(q, comp[m, span])
        total = lax.fori_loop(0, tiles, body, jnp.zeros((rank, cols), F32), unroll=4)
        right_all[m, dp] = total.astype(BF16)
        for k in range(1, n_dp):
            send(right_all.at[m, dp], right_all.at[m, dp], r_send.at[m, k], r_recv.at[m, dp],
                 (lax.rem(dp + k, n_dp), z))

    def right_finish(m):
        for k in range(1, n_dp):
            source = lax.rem(dp + k, n_dp)
            landed(right_all.at[m, source], r_send.at[m, k], r_recv.at[m, source])
        total = right_all[m, 0].astype(F32)
        for c in range(1, n_dp):
            total = total + right_all[m, c].astype(F32)
        right_low_ref[m] = (total * (1.0 / n_dp)).astype(BF16)

    pairs = [(core_finish, chip_start), (chip_finish, z_start), (z_finish, z_gather_start),
             (z_gather_finish, chip_gather_start), (chip_gather_finish, core_gather_start)]

    def advance(m, stage):
        for step in pairs[stage]:
            step(m)

    compensate(0, 0, tiles)
    core_start(0)
    compensate(1, 0, tiles // 2)
    advance(0, 0)
    compensate(1, tiles // 2, tiles)
    core_start(1)
    advance(0, 1)
    advance(1, 0)
    advance(0, 2)
    advance(1, 1)
    advance(0, 3)
    advance(1, 2)
    inverse_0 = inverse_factor(0)
    advance(0, 4)
    advance(1, 3)
    core_gather_finish(0)
    project(0, inverse_0)
    advance(1, 4)
    inverse_1 = inverse_factor(1)
    core_gather_finish(1)
    project(1, inverse_1)
    right_finish(0)
    right_finish(1)
    for copy in sent:
        copy.wait_send()


def residue_kernel(comp, q_low, right_ref, feed_hbm, update_hbm, out, update, store_sem, update_sem):
    mats, tiles, _, tile = q_low.shape
    piece = min(tile, 2 * LANES)
    dp = lax.axis_index("dp")

    def store(m, t):
        span = pl.ds(t * tile, tile)
        return pltpu.make_async_copy(out.at[m, span], feed_hbm.at[0, m, span], store_sem.at[m, t])

    for m in range(mats):
        right = right_ref[m]

        def body(t, carry, m=m, right=right):
            for r in range(0, tile, piece):
                approx = tn_dot(q_low[m, t, :, r:r + piece], right)
                rows = pl.ds(pl.multiple_of(t * tile + r, piece), piece)
                out[m, rows] = (comp[m, rows].astype(F32) - approx).astype(BF16)
            store(m, t).start()
            return carry
        lax.fori_loop(0, tiles, body, 0, unroll=4)
    for m in range(mats):
        for r in range(0, tile, piece):
            update[m, r:r + piece] = tn_dot(q_low[m, dp, :, r:r + piece], right_ref[m]).astype(BF16)
    update_copy = pltpu.make_async_copy(update, update_hbm, update_sem)
    update_copy.start()
    for m in range(mats):
        def finish(t, carry, m=m):
            store(m, t).wait()
            return carry
        lax.fori_loop(0, tiles, finish, 0)
    update_copy.wait()


def shards(n_dp, n_mp, gradients, feedback, right_factor):
    _, mats, rows, cols = gradients.shape
    rank = right_factor.shape[2]
    tile = rows // n_dp
    tiles = rows // tile
    blocks = rows // LANES
    half_blocks = blocks // CORES
    chips = n_dp // CORES
    chip_blocks = half_blocks // chips
    z_blocks = chip_blocks // n_mp if chip_blocks % n_mp == 0 else chip_blocks
    dma = pltpu.SemaphoreType.DMA
    any_spec = pl.BlockSpec(memory_space=pl.ANY)
    vmem_spec = pl.BlockSpec(memory_space=pltpu.VMEM)
    comp, q_low, right_low = pl.pallas_call(
        functools.partial(reduce_kernel, n_dp, n_mp),
        out_shape=(
            jax.ShapeDtypeStruct((mats, rows, cols), BF16),
            jax.ShapeDtypeStruct((mats, tiles, rank, tile), BF16),
            jax.ShapeDtypeStruct((mats, rank, cols), BF16),
        ),
        in_specs=[any_spec, any_spec, vmem_spec],
        out_specs=(vmem_spec, vmem_spec, vmem_spec),
        scratch_shapes=[
            pltpu.VMEM((mats, rows, cols), BF16),
            pltpu.VMEM((mats, blocks, rank, LANES), F32),
            pltpu.VMEM((mats, half_blocks, rank, LANES), F32),
            pltpu.VMEM((mats, half_blocks, rank, LANES), BF16),
            pltpu.VMEM((mats, half_blocks, rank, LANES), F32),
            pltpu.VMEM((mats, chips, chip_blocks, rank, LANES), BF16),
            pltpu.VMEM((mats, chip_blocks, rank, LANES), F32),
            pltpu.VMEM((mats, chip_blocks, rank, LANES), BF16),
            pltpu.VMEM((mats, n_mp, z_blocks, rank, LANES), BF16),
            pltpu.VMEM((mats, blocks, rank, LANES), F32),
            pltpu.VMEM((mats, n_dp, rank, LANES), F32),
            pltpu.VMEM((mats, n_dp, rank, cols), BF16),
            dma((2, mats, tiles)),
            dma((mats,)), dma((mats,)), dma((mats, chips)), dma((mats, chips)),
            dma((mats, n_mp)), dma((mats, n_mp)),
            dma((mats, n_mp)), dma((mats, n_mp)), dma((mats, chips)), dma((mats, chips)),
            dma((mats,)), dma((mats,)),
            dma((mats, n_dp)), dma((mats, n_dp)), dma((mats, n_dp)), dma((mats, n_dp)),
        ],
        compiler_params=pltpu.CompilerParams(
            collective_id=0, has_side_effects=True, vmem_limit_bytes=44 * 1024 * 1024),
        name="reduce_factors",
    )(gradients, feedback, jnp.swapaxes(right_factor, 1, 2))
    return pl.pallas_call(
        residue_kernel,
        out_shape=(
            jax.ShapeDtypeStruct((1, mats, rows, cols), BF16),
            jax.ShapeDtypeStruct((mats, tile, cols), BF16),
        ),
        in_specs=[vmem_spec, vmem_spec, vmem_spec],
        out_specs=(any_spec, any_spec),
        scratch_shapes=[
            pltpu.VMEM((mats, rows, cols), BF16),
            pltpu.VMEM((mats, tile, cols), BF16),
            dma((mats, tiles)), dma,
        ],
        compiler_params=pltpu.CompilerParams(vmem_limit_bytes=24 * 1024 * 1024),
        name="subtract_approx",
    )(comp, q_low, right_low)


def solution(mesh):
    return jax.shard_map(
        functools.partial(shards, mesh.shape["dp"], mesh.shape["mp"]),
        mesh=mesh,
        in_specs=(P("dp", None, None, "mp"), P("dp", None, None, "mp"), P(None, "mp", None)),
        out_specs=(P("dp", None, None, "mp"), P(None, "dp", "mp")),
        check_vma=False,
    )
```
